32 devices in a mesh: seq: 8 (over z, y), chan: 4 (over x, core).
Axes of the slice: x: 2, y: 2, z: 4, core: 2. Of those that a mesh axis runs over, the one named last changes fastest.
Arguments:
- queries: bfloat16 [1024, 8192], P('seq', 'chan'), may hold values from -6 to 6
- key_in: bfloat16 [1024, 8192], P('seq', 'chan'), may hold values from -6 to 6
- values: bfloat16 [1024, 8192], P('seq', 'chan'), may hold values from -6 to 6
- decay_rates: float32 [8192], P('chan'), may hold values from 9.765625e-05 to 0.03
- skip_gain: float32 [8192], P('chan'), may hold values from -4 to 4
- out_gain: float32 [8192], P('chan'), may hold values from 0.5 to 1.5
- pos_weight: float32 [32, 64], replicated, may hold values from -1.5 to 1.5
- filt_weight: float32 [64, 8192], P(None, 'chan'), may hold values from -0.75 to 0.75
Outputs:
- layer_out: float32 [1024, 8192], P('seq', 'chan')
The draws below stay inside these ranges and needn't reach their ends.
All inputs are finite; a program needn't handle non-finite values.
Results may differ from the reference program's by a relative error of at most 0.0075.
Values may be sent and summed in bfloat16 or wider, within the bound.
A program may use at most 128 MiB of HBM per device.

```python
import math
import jax
import jax.numpy as jnp
import numpy as np
from jax import lax

D = 8192
FREQS = 16
FILTER_HID = 64
FEATS = 32
SEQ = 1024


def shard_levels(stream_key, shape, cuts, smallest, high):
    def one(dim, shards_of):
        heights = jax.random.uniform(jax.random.fold_in(jax.random.fold_in(stream_key, 6), dim), (shards_of,), jnp.float32, smallest / len(cuts), high / len(cuts))
        return jnp.repeat(jnp.exp(heights), shape[dim] // shards_of).reshape((-1,) + (1,) * (len(shape) - dim - 1))

    level = one(*cuts[0])
    for cut in cuts[1:]:
        level = level * one(*cut)
    return level


def scatter_about(stream_key, dims, spread, limit, cuts=(), held_as=jnp.bfloat16):
    loudness = shard_levels(stream_key, dims, cuts, -0.22, 0.18) if cuts else 1.0
    result = jax.random.normal(stream_key, dims, jnp.float32) * spread * loudness
    return jnp.minimum(jnp.maximum(result, -limit), limit).astype(held_as)


def setup_inputs(seed: int = 0) -> dict:
    seeds = jax.random.split(jax.random.key(seed), 9)
    queries = scatter_about(seeds[0], (SEQ, D), 1.0, 6.0, ((0, 8), (1, 4)))
    key_in = scatter_about(seeds[1], (SEQ, D), 1.0, 6.0, ((0, 8), (1, 4)))
    values = scatter_about(seeds[2], (SEQ, D), 1.0, 6.0, ((0, 8), (1, 4)))
    decay_rates = jnp.clip(jnp.exp(math.log(0.03) - 5.727499 * jax.random.uniform(seeds[3], (D,), jnp.float32) ** shard_levels(seeds[3], (D,), ((0, 4),), -0.2, 0.2)), 9.765625145519152e-05, 0.03)
    skip_gain = scatter_about(seeds[4], (D,), 1.0, 4.0, ((0, 4),), jnp.float32)
    out_gain = jnp.clip(1.0 + 0.1 * jax.random.normal(seeds[5], (D,), jnp.float32), 0.5, 1.5)
    pos_weight = scatter_about(seeds[6], (FEATS, FILTER_HID), FREQS ** -0.5, 1.5, (), jnp.float32)
    filt_weight = scatter_about(seeds[7], (FILTER_HID, D), FILTER_HID ** -0.5, 0.75, ((1, 4),), jnp.float32)
    return {"queries": queries, "key_in": key_in, "values": values, "decay_rates": decay_rates, "skip_gain": skip_gain, "out_gain": out_gain, "pos_weight": pos_weight, "filt_weight": filt_weight}


def wave_table():
    return np.array([int(4096 * 2.0 ** (-e / 2.0)) for e in range(FREQS)], dtype=np.int32)

def features(position_grid):
    wave_numbers = jnp.asarray(wave_table())
    phases = position_grid[:, None] * wave_numbers[None, :] % 8192
    angles = phases.astype(jnp.float32) * (2.0 * math.pi / 8192.0)
    return jnp.concatenate([jnp.sin(angles), jnp.cos(angles)], axis=1)

def reference(queries, key_in, values, decay_rates, skip_gain, out_gain, pos_weight, filt_weight):
    position_grid = jnp.arange(SEQ, dtype=jnp.int32)
    hidden = jnp.tanh(jnp.dot(features(position_grid), pos_weight, precision=lax.Precision.HIGHEST))
    time_points = position_grid.astype(jnp.float32)[:, None]
    mixed_kv = (key_in.astype(jnp.float32) * values.astype(jnp.float32)).astype(jnp.bfloat16)
    group_width = math.gcd(D, 512)

    def group_out(group_index):
        group_start = (group_index * group_width).astype(jnp.int32)
        rate_factor = lax.dynamic_slice_in_dim(decay_rates, group_start, group_width)
        weight_part = lax.dynamic_slice_in_dim(filt_weight, group_start, group_width, 1)
        data_part = lax.dynamic_slice_in_dim(mixed_kv, group_start, group_width, 1).astype(jnp.float32)
        query_part = lax.dynamic_slice_in_dim(queries, group_start, group_width, 1).astype(jnp.float32)
        skip_part = lax.dynamic_slice_in_dim(skip_gain, group_start, group_width)
        filter_envelope = jnp.dot(hidden, weight_part, precision=lax.Precision.HIGHEST)
        filter_exact = jnp.exp(-rate_factor[None, :] * time_points) * jnp.sqrt(2.0 * rate_factor)[None, :] * filter_envelope
        filter_taps = lax.optimization_barrier(filter_exact.astype(jnp.bfloat16)).astype(jnp.float32)
        spectrum = jnp.fft.rfft(filter_taps, n=2 * SEQ, axis=0) * jnp.fft.rfft(data_part, n=2 * SEQ, axis=0)
        long_conv = jnp.fft.irfft(spectrum, n=2 * SEQ, axis=0)[:SEQ]
        return query_part * (long_conv + skip_part[None, :] * data_part)
    pieces = lax.map(group_out, jnp.arange(D // group_width, dtype=jnp.int32))
    gated = jnp.transpose(pieces, (1, 0, 2)).reshape(SEQ, D)
    inv_rms = lax.rsqrt(lax.optimization_barrier(jnp.mean(gated * gated, axis=1, keepdims=True)) + 1e-06)
    return gated * inv_rms * out_gain[None, :]
```

```python
import functools
import math

import jax
import jax.numpy as jnp
import numpy as np
from jax import lax
from jax.experimental import pallas as pl
from jax.experimental.pallas import tpu as pltpu
from jax.sharding import PartitionSpec as P

FREQS = 16
LANES = 128
HIGHEST = lax.Precision.HIGHEST
MESH = pl.DeviceIdType.MESH


def feature_table(length):
    waves = np.array([int(4096 * 2.0 ** (-e / 2.0)) for e in range(FREQS)], dtype=np.int64)
    phases = np.arange(length, dtype=np.int64)[:, None] * waves[None, :] % 8192
    angles = phases * (2.0 * math.pi / 8192.0)
    return np.concatenate([np.sin(angles), np.cos(angles)], axis=1).astype(np.float32)


def spectral_tables(length, block):
    k = np.arange(length, dtype=np.int64)
    turns = (2 * k[:, None] + 1) * k[None, :] % (4 * length)
    angles = turns * (math.pi / (2 * length))
    both = np.stack([np.cos(angles), np.sin(angles)]).reshape(2, length // block, block, length)
    forward = both.transpose(1, 0, 2, 3).reshape(2 * length, length)
    backward = forward.T / length
    return forward.astype(jnp.bfloat16), backward.astype(jnp.bfloat16)


def plain(queries, key_in, values, decay_rates, skip_gain, out_gain, pos_weight, filt_weight):
    rows, cols = queries.shape
    seq_count = lax.axis_size("seq")
    length, width = rows * seq_count, cols // seq_count
    forward, backward = (jnp.asarray(t) for t in spectral_tables(length, length))
    mixed = (key_in.astype(jnp.float32) * values.astype(jnp.float32)).astype(jnp.bfloat16)
    data = lax.all_to_all(mixed, "seq", 1, 0, tiled=True)
    start = lax.axis_index("seq") * width
    rates = lax.dynamic_slice_in_dim(decay_rates, start, width)
    weights = lax.dynamic_slice_in_dim(filt_weight, start, width, 1)
    hidden = jnp.tanh(jnp.dot(jnp.asarray(feature_table(length)), pos_weight, precision=HIGHEST))
    profile = jnp.dot(hidden, weights, precision=HIGHEST)
    time = jnp.arange(length, dtype=jnp.float32)[:, None]
    taps = (jnp.exp(-rates[None, :] * time) * jnp.sqrt(2.0 * rates)[None, :] * profile).astype(jnp.bfloat16)
    filt_spec = jnp.dot(forward, taps, preferred_element_type=jnp.float32)
    data_spec = jnp.dot(forward, data, preferred_element_type=jnp.float32)
    fc, fs, dc, ds = filt_spec[:length], filt_spec[length:], data_spec[:length], data_spec[length:]
    spec = jnp.concatenate([fc * dc - fs * ds, fc * ds + fs * dc], axis=0).astype(jnp.bfloat16)
    conv = jnp.dot(backward, spec, preferred_element_type=jnp.float32).astype(jnp.bfloat16)
    conv = lax.all_to_all(conv, "seq", 0, 1, tiled=True).astype(jnp.float32)
    gated = queries.astype(jnp.float32) * (conv + skip_gain[None, :] * mixed.astype(jnp.float32))
    row_sums = lax.psum(jnp.sum(gated * gated, axis=1), "chan")
    inv_rms = lax.rsqrt(row_sums / (cols * lax.axis_size("chan")) + 1e-06)
    return gated * inv_rms[:, None] * out_gain[None, :]


def solution(mesh):
    in_specs = (
        P("seq", "chan"),
        P("seq", "chan"),
        P("seq", "chan"),
        P("chan"),
        P("chan"),
        P("chan"),
        P(),
        P(None, "chan"),
    )
    return jax.shard_map(
        plain, mesh=mesh, in_specs=in_specs, out_specs=P("seq", "chan"), check_vma=False
    )
```

```python
import functools
import math

import jax
import jax.numpy as jnp
import numpy as np
from jax import lax
from jax.experimental import pallas as pl
from jax.experimental.pallas import tpu as pltpu
from jax.sharding import PartitionSpec as P

FREQS = 16
LANES = 128
HIGHEST = lax.Precision.HIGHEST
MESH = pl.DeviceIdType.MESH


def feature_table(length):
    waves = np.array([int(4096 * 2.0 ** (-e / 2.0)) for e in range(FREQS)], dtype=np.int64)
    phases = np.arange(length, dtype=np.int64)[:, None] * waves[None, :] % 8192
    angles = phases * (2.0 * math.pi / 8192.0)
    return np.concatenate([np.sin(angles), np.cos(angles)], axis=1).astype(np.float32)


def spectral_tables(length, block):
    k = np.arange(length, dtype=np.int64)
    turns = (2 * k[:, None] + 1) * k[None, :] % (4 * length)
    angles = turns * (math.pi / (2 * length))
    both = np.stack([np.cos(angles), np.sin(angles)]).reshape(2, length // block, block, length)
    forward = both.transpose(1, 0, 2, 3).reshape(2 * length, length)
    backward = forward.T / length
    return forward.astype(jnp.bfloat16), backward.astype(jnp.bfloat16)


def plain(queries, key_in, values, decay_rates, skip_gain, out_gain, pos_weight, filt_weight):
    rows, cols = queries.shape
    seq_count = lax.axis_size("seq")
    length, width = rows * seq_count, cols // seq_count
    forward, backward = (jnp.asarray(t) for t in spectral_tables(length, length))
    mixed = (key_in.astype(jnp.float32) * values.astype(jnp.float32)).astype(jnp.bfloat16)
    data = lax.all_to_all(mixed, "seq", 1, 0, tiled=True)
    start = lax.axis_index("seq") * width
    rates = lax.dynamic_slice_in_dim(decay_rates, start, width)
    weights = lax.dynamic_slice_in_dim(filt_weight, start, width, 1)
    hidden = jnp.tanh(jnp.dot(jnp.asarray(feature_table(length)), pos_weight, precision=HIGHEST))
    profile = jnp.dot(hidden, weights, precision=HIGHEST)
    time = jnp.arange(length, dtype=jnp.float32)[:, None]
    taps = (jnp.exp(-rates[None, :] * time) * jnp.sqrt(2.0 * rates)[None, :] * profile).astype(jnp.bfloat16)
    filt_spec = jnp.dot(forward, taps, preferred_element_type=jnp.float32)
    data_spec = jnp.dot(forward, data, preferred_element_type=jnp.float32)
    fc, fs, dc, ds = filt_spec[:length], filt_spec[length:], data_spec[:length], data_spec[length:]
    spec = jnp.concatenate([fc * dc - fs * ds, fc * ds + fs * dc], axis=0).astype(jnp.bfloat16)
    conv = jnp.dot(backward, spec, preferred_element_type=jnp.float32).astype(jnp.bfloat16)
    conv = lax.all_to_all(conv, "seq", 0, 1, tiled=True).astype(jnp.float32)
    gated = queries.astype(jnp.float32) * (conv + skip_gain[None, :] * mixed.astype(jnp.float32))
    row_sums = lax.psum(jnp.sum(gated * gated, axis=1), "chan")
    inv_rms = lax.rsqrt(row_sums / (cols * lax.axis_size("chan")) + 1e-06)
    return gated * inv_rms[:, None] * out_gain[None, :]


def kernel(
    n, m, block,
    q_hbm, k_hbm, v_hbm, rates_ref, skip_ref, feats_ref, pos_ref, weight_hbm, fwd_hbm, bwd_hbm,
    gated_ref, inv_ref,
    q_buf, k_buf, v_buf, weight_buf, fwd_buf, bwd_buf,
    mixed, data, taps, filt_spec, spec, conv, back, sums_out, sums_in,
    in_sem, send1, recv1, send2, recv2, send3, recv3,
):
    rows, cols = q_buf.shape
    length, width = taps.shape
    chunks = width // LANES
    me, lane = lax.axis_index("seq"), lax.axis_index("chan")
    order = sorted(range(1, n), key=lambda k: abs(k - n // 2))

    def seq_peer(k):
        return lax.rem(me + k, n)

    barrier = pltpu.get_barrier_semaphore()
    for k in range(1, n):
        pl.semaphore_signal(barrier, inc=1, device_id=(seq_peer(k), lane), device_id_type=MESH)
    for k in range(1, m):
        pl.semaphore_signal(barrier, inc=1, device_id=(me, lax.rem(lane + k, m)), device_id_type=MESH)

    own = pl.ds(pl.multiple_of(me * width, LANES), width)
    loads = [
        pltpu.make_async_copy(k_hbm, k_buf, in_sem.at[0]),
        pltpu.make_async_copy(v_hbm, v_buf, in_sem.at[1]),
        pltpu.make_async_copy(weight_hbm.at[:, own], weight_buf, in_sem.at[2]),
        pltpu.make_async_copy(fwd_hbm, fwd_buf, in_sem.at[3]),
        pltpu.make_async_copy(bwd_hbm, bwd_buf, in_sem.at[4]),
        pltpu.make_async_copy(q_hbm, q_buf, in_sem.at[5]),
    ]
    for load in loads:
        load.start()
    loads[0].wait()
    loads[1].wait()

    @pl.loop(0, n)
    def _(d):
        for c in range(chunks):
            at = pl.ds(pl.multiple_of(d * width + c * LANES, LANES), LANES)
            product = k_buf[:, at].astype(jnp.float32) * v_buf[:, at].astype(jnp.float32)
            mixed[c, d] = product.astype(jnp.bfloat16)

    pl.semaphore_wait(barrier, n - 1 + m - 1)

    def out_copy(c, k):
        peer = seq_peer(k)
        return pltpu.make_async_remote_copy(
            src_ref=mixed.at[c, peer], dst_ref=data.at[c, me],
            send_sem=send1.at[c, peer], recv_sem=recv1.at[c, me],
            device_id=(peer, lane), device_id_type=MESH,
        )

    def in_copy(c, k):
        peer = seq_peer(k)
        return pltpu.make_async_remote_copy(
            src_ref=mixed.at[c, peer], dst_ref=data.at[c, peer],
            send_sem=send1.at[c, peer], recv_sem=recv1.at[c, peer],
            device_id=(peer, lane), device_id_type=MESH,
        )

    def out_back(c, peer):
        return pltpu.make_async_remote_copy(
            src_ref=conv.at[c, peer], dst_ref=back.at[c, me],
            send_sem=send2.at[c, peer], recv_sem=recv2.at[c, me],
            device_id=(peer, lane), device_id_type=MESH,
        )

    def in_back(c, peer):
        return pltpu.make_async_remote_copy(
            src_ref=conv.at[c, peer], dst_ref=back.at[c, peer],
            send_sem=send2.at[c, peer], recv_sem=recv2.at[c, peer],
            device_id=(peer, lane), device_id_type=MESH,
        )

    for c in range(chunks):
        for k in order:
            out_copy(c, k).start()
    for c in range(chunks):
        data[c, me] = mixed[c, me]

    hidden = jnp.tanh(jnp.dot(feats_ref[...], pos_ref[...], precision=HIGHEST, preferred_element_type=jnp.float32))
    loads[2].wait()
    rates = rates_ref[:, own]
    gain = jnp.sqrt(2.0 * rates)
    for i in range(n):
        part = hidden[i * rows:(i + 1) * rows]
        profile = jnp.dot(part, weight_buf[...], precision=HIGHEST, preferred_element_type=jnp.float32)
        time = (lax.broadcasted_iota(jnp.int32, (rows, width), 0) + i * rows).astype(jnp.float32)
        taps[pl.ds(i * rows, rows), :] = (jnp.exp(-rates * time) * gain * profile).astype(jnp.bfloat16)
    loads[3].wait()

    @pl.loop(0, length // block)
    def _(b):
        at = pl.ds(pl.multiple_of(b * 2 * block, 2 * block), 2 * block)
        filt_spec[at, :] = jnp.dot(fwd_buf[at, :], taps[...], preferred_element_type=jnp.float32)

    loads[4].wait()
    for c in range(chunks):
        for k in order:
            in_copy(c, k).wait_recv()
        held = data.at[c]

        @pl.loop(0, length // block)
        def _(b):
            at = pl.ds(pl.multiple_of(b * 2 * block, 2 * block), 2 * block)
            x = jnp.dot(fwd_buf[at, :], held[...].reshape(length, LANES), preferred_element_type=jnp.float32)
            h = filt_spec[at, pl.ds(c * LANES, LANES)]
            xc, xs, hc, hs = x[:block], x[block:], h[:block], h[block:]
            both = jnp.concatenate([xc * hc - xs * hs, xc * hs + xs * hc], axis=0)
            spec[at, :] = both.astype(jnp.bfloat16)

        pairs = n // 2
        for step in [(pairs // 2 + i) % pairs for i in range(pairs)]:
            pair = lax.rem(me // 2 + step, pairs)
            at = pl.ds(pl.multiple_of(pair * 2 * rows, 2 * rows), 2 * rows)
            part = jnp.dot(bwd_buf[at, :], spec[...], preferred_element_type=jnp.float32)
            conv[c, pl.ds(pair * 2, 2)] = part.astype(jnp.bfloat16).reshape(2, rows, LANES)
            if step:
                for half in range(2):
                    out_back(c, pair * 2 + half).start()
            else:
                out_back(c, pair * 2 + 1 - lax.rem(me, 2)).start()
        back[c, me] = conv[c, me]

    loads[5].wait()
    squares = jnp.zeros((rows, LANES), jnp.float32)
    for c in range(chunks):
        for k in [0] + order[::-1]:
            peer = seq_peer(k)
            if k:
                in_back(c, peer).wait_recv()
            at = pl.ds(pl.multiple_of(peer * width + c * LANES, LANES), LANES)
            total = back[c, peer].astype(jnp.float32) + skip_ref[:, at] * mixed[c, peer].astype(jnp.float32)
            gated = q_buf[:, at].astype(jnp.float32) * total
            gated_ref[:, at] = gated
            squares = squares + gated * gated
    eye = lax.broadcasted_iota(jnp.int32, (rows, LANES), 0) == lax.broadcasted_iota(jnp.int32, (rows, LANES), 1)
    column = jnp.sum(squares, axis=1, keepdims=True)
    line = jnp.sum(jnp.where(eye, column, 0.0), axis=0, keepdims=True)
    sums_out[...] = jnp.broadcast_to(line, sums_out.shape)

    def sums_copy(k, mine):
        peer = lax.rem(lane + k, m)
        slot = lane if mine else peer
        return pltpu.make_async_remote_copy(
            src_ref=sums_out, dst_ref=sums_in.at[slot],
            send_sem=send3.at[peer], recv_sem=recv3.at[slot],
            device_id=(me, peer), device_id_type=MESH,
        )

    for k in range(1, m):
        sums_copy(k, True).start()
    total = sums_out[...]
    for k in range(1, m):
        sums_copy(k, False).wait_recv()
        total = total + sums_in[lax.rem(lane + k, m)]
    inv = lax.rsqrt(total[:1] / (cols * m) + 1e-06)
    inv_ref[...] = jnp.sum(jnp.where(eye, inv, 0.0), axis=1, keepdims=True)

    for c in range(chunks):
        for k in order:
            out_copy(c, k).wait_send()
            out_back(c, seq_peer(k)).wait_send()
    for k in range(1, m):
        sums_copy(k, True).wait_send()


def fused(queries, key_in, values, decay_rates, skip_gain, out_gain, pos_weight, filt_weight):
    rows, cols = queries.shape
    n, m = lax.axis_size("seq"), lax.axis_size("chan")
    length, width = rows * n, cols // n
    chunks = width // LANES
    block = min(LANES, length)
    forward, backward = (jnp.asarray(t) for t in spectral_tables(length, block))
    vmem = pl.BlockSpec(memory_space=pltpu.VMEM)
    hbm = pl.BlockSpec(memory_space=pl.ANY)
    bf16, f32 = jnp.bfloat16, jnp.float32
    dma = pltpu.SemaphoreType.DMA
    gated, inv = pl.pallas_call(
        functools.partial(kernel, n, m, block),
        out_shape=(
            jax.ShapeDtypeStruct((rows, cols), f32),
            jax.ShapeDtypeStruct((rows, 1), f32),
        ),
        in_specs=[hbm, hbm, hbm, vmem, vmem, vmem, vmem, hbm, hbm, hbm],
        out_specs=(vmem, vmem),
        scratch_shapes=[
            pltpu.VMEM((rows, cols), bf16),
            pltpu.VMEM((rows, cols), bf16),
            pltpu.VMEM((rows, cols), bf16),
            pltpu.VMEM((filt_weight.shape[0], width), f32),
            pltpu.VMEM((2 * length, length), bf16),
            pltpu.VMEM((length, 2 * length), bf16),
            pltpu.VMEM((chunks, n, rows, LANES), bf16),
            pltpu.VMEM((chunks, n, rows, LANES), bf16),
            pltpu.VMEM((length, width), bf16),
            pltpu.VMEM((2 * length, width), f32),
            pltpu.VMEM((2 * length, LANES), bf16),
            pltpu.VMEM((chunks, n, rows, LANES), bf16),
            pltpu.VMEM((chunks, n, rows, LANES), bf16),
            pltpu.VMEM((8, LANES), f32),
            pltpu.VMEM((m, 8, LANES), f32),
            dma((6,)),
            dma((chunks, n)),
            dma((chunks, n)),
            dma((chunks, n)),
            dma((chunks, n)),
            dma((m,)),
            dma((m,)),
        ],
        compiler_params=pltpu.CompilerParams(
            collective_id=0, has_side_effects=True, vmem_limit_bytes=40 * 1024 * 1024
        ),
    )(
        queries, key_in, values, decay_rates[None, :], skip_gain[None, :],
        jnp.asarray(feature_table(length)), pos_weight, filt_weight, forward, backward,
    )
    return gated * inv * out_gain[None, :]


def local(queries, *others):
    rows, cols = queries.shape
    n = lax.axis_size("seq")
    if rows == LANES and n % 4 == 0 and cols % (LANES * n) == 0:
        return fused(queries, *others)
    return plain(queries, *others)


def solution(mesh):
    in_specs = (
        P("seq", "chan"),
        P("seq", "chan"),
        P("seq", "chan"),
        P("chan"),
        P("chan"),
        P("chan"),
        P(),
        P(None, "chan"),
    )
    return jax.shard_map(
        local, mesh=mesh, in_specs=in_specs, out_specs=P("seq", "chan"), check_vma=False
    )
```

```python
import functools
import math

import jax
import jax.numpy as jnp
import numpy as np
from jax import lax
from jax.experimental import pallas as pl
from jax.experimental.pallas import tpu as pltpu
from jax.sharding import PartitionSpec as P

FREQS = 16
LANES = 128
HIGHEST = lax.Precision.HIGHEST
MESH = pl.DeviceIdType.MESH


def feature_table(length):
    waves = np.array([int(4096 * 2.0 ** (-e / 2.0)) for e in range(FREQS)], dtype=np.int64)
    phases = np.arange(length, dtype=np.int64)[:, None] * waves[None, :] % 8192
    angles = phases * (2.0 * math.pi / 8192.0)
    return np.concatenate([np.sin(angles), np.cos(angles)], axis=1).astype(np.float32)


def spectral_tables(length, block):
    k = np.arange(length, dtype=np.int64)
    turns = (2 * k[:, None] + 1) * k[None, :] % (4 * length)
    angles = turns * (math.pi / (2 * length))
    both = np.stack([np.cos(angles), np.sin(angles)]).reshape(2, length // block, block, length)
    forward = both.transpose(1, 0, 2, 3).reshape(2 * length, length)
    backward = forward.T / length
    return forward.astype(jnp.bfloat16), backward.astype(jnp.bfloat16)


def plain(queries, key_in, values, decay_rates, skip_gain, out_gain, pos_weight, filt_weight):
    rows, cols = queries.shape
    seq_count = lax.axis_size("seq")
    length, width = rows * seq_count, cols // seq_count
    forward, backward = (jnp.asarray(t) for t in spectral_tables(length, length))
    mixed = (key_in.astype(jnp.float32) * values.astype(jnp.float32)).astype(jnp.bfloat16)
    data = lax.all_to_all(mixed, "seq", 1, 0, tiled=True)
    start = lax.axis_index("seq") * width
    rates = lax.dynamic_slice_in_dim(decay_rates, start, width)
    weights = lax.dynamic_slice_in_dim(filt_weight, start, width, 1)
    hidden = jnp.tanh(jnp.dot(jnp.asarray(feature_table(length)), pos_weight, precision=HIGHEST))
    profile = jnp.dot(hidden, weights, precision=HIGHEST)
    time = jnp.arange(length, dtype=jnp.float32)[:, None]
    taps = (jnp.exp(-rates[None, :] * time) * jnp.sqrt(2.0 * rates)[None, :] * profile).astype(jnp.bfloat16)
    filt_spec = jnp.dot(forward, taps, preferred_element_type=jnp.float32)
    data_spec = jnp.dot(forward, data, preferred_element_type=jnp.float32)
    fc, fs, dc, ds = filt_spec[:length], filt_spec[length:], data_spec[:length], data_spec[length:]
    spec = jnp.concatenate([fc * dc - fs * ds, fc * ds + fs * dc], axis=0).astype(jnp.bfloat16)
    conv = jnp.dot(backward, spec, preferred_element_type=jnp.float32).astype(jnp.bfloat16)
    conv = lax.all_to_all(conv, "seq", 0, 1, tiled=True).astype(jnp.float32)
    gated = queries.astype(jnp.float32) * (conv + skip_gain[None, :] * mixed.astype(jnp.float32))
    row_sums = lax.psum(jnp.sum(gated * gated, axis=1), "chan")
    inv_rms = lax.rsqrt(row_sums / (cols * lax.axis_size("chan")) + 1e-06)
    return gated * inv_rms[:, None] * out_gain[None, :]


def kernel(
    n, m, block,
    q_hbm, k_hbm, v_hbm, rates_hbm, skip_hbm, gain_hbm, feats_hbm, pos_hbm, weight_hbm, fwd_hbm, bwd_hbm,
    out_hbm,
    q_buf, k_buf, v_buf, rates_ref, skip_ref, gain_ref, feats_ref, pos_ref, weight_buf, fwd_buf, bwd_buf,
    mixed, data, taps, filt_spec, spec, conv, back, sums_out, sums_in,
    gated_ref, in_sem, key_sem, value_sem, out_sem, send1, recv1, send2, recv2, send3, recv3,
):
    rows, cols = q_buf.shape
    length, width = taps.shape
    chunks = width // LANES
    me, lane = lax.axis_index("seq"), lax.axis_index("chan")
    order = sorted(range(1, n), key=lambda k: abs(k - n // 2))

    def seq_peer(k):
        return lax.rem(me + k, n)

    barrier = pltpu.get_barrier_semaphore()
    for k in range(1, n):
        pl.semaphore_signal(barrier, inc=1, device_id=(seq_peer(k), lane), device_id_type=MESH)
    for k in range(1, m):
        pl.semaphore_signal(barrier, inc=1, device_id=(me, lax.rem(lane + k, m)), device_id_type=MESH)

    own = pl.ds(pl.multiple_of(me * width, LANES), width)
    def piece(k):
        return pl.ds(pl.multiple_of(seq_peer(k) * width, LANES), width)

    pieces = order + [0]
    firsts = [
        (
            pltpu.make_async_copy(k_hbm.at[:, piece(k)], k_buf.at[:, piece(k)], key_sem.at[k]),
            pltpu.make_async_copy(v_hbm.at[:, piece(k)], v_buf.at[:, piece(k)], value_sem.at[k]),
        )
        for k in pieces
    ]
    for pair in firsts:
        for load in pair:
            load.start()
    loads = [
        pltpu.make_async_copy(feats_hbm, feats_ref, in_sem.at[0]),
        pltpu.make_async_copy(pos_hbm, pos_ref, in_sem.at[1]),
        pltpu.make_async_copy(rates_hbm.at[:, own], rates_ref, in_sem.at[2]),
        pltpu.make_async_copy(weight_hbm.at[:, own], weight_buf, in_sem.at[3]),
        pltpu.make_async_copy(fwd_hbm, fwd_buf, in_sem.at[4]),
        pltpu.make_async_copy(bwd_hbm, bwd_buf, in_sem.at[5]),
        pltpu.make_async_copy(skip_hbm, skip_ref, in_sem.at[6]),
        pltpu.make_async_copy(q_hbm, q_buf, in_sem.at[7]),
        pltpu.make_async_copy(gain_hbm, gain_ref, in_sem.at[8]),
    ]

    def mix(i):
        for load in firsts[i]:
            load.wait()
        d = seq_peer(pieces[i])
        for c in range(chunks):
            at = pl.ds(pl.multiple_of(d * width + c * LANES, LANES), LANES)
            product = k_buf[:, at].astype(jnp.float32) * v_buf[:, at].astype(jnp.float32)
            mixed[c, d] = product.astype(jnp.bfloat16)

    mix(0)
    pl.semaphore_wait(barrier, n - 1 + m - 1)

    def out_copy(c, k):
        peer = seq_peer(k)
        return pltpu.make_async_remote_copy(
            src_ref=mixed.at[c, peer], dst_ref=data.at[c, me],
            send_sem=send1.at[c, peer], recv_sem=recv1.at[c, me],
            device_id=(peer, lane), device_id_type=MESH,
        )

    def in_copy(c, k):
        peer = seq_peer(k)
        return pltpu.make_async_remote_copy(
            src_ref=mixed.at[c, peer], dst_ref=data.at[c, peer],
            send_sem=send1.at[c, peer], recv_sem=recv1.at[c, peer],
            device_id=(peer, lane), device_id_type=MESH,
        )

    def out_back(c, peer):
        return pltpu.make_async_remote_copy(
            src_ref=conv.at[c, peer], dst_ref=back.at[c, me],
            send_sem=send2.at[c, peer], recv_sem=recv2.at[c, me],
            device_id=(peer, lane), device_id_type=MESH,
        )

    def in_back(c, peer):
        return pltpu.make_async_remote_copy(
            src_ref=conv.at[c, peer], dst_ref=back.at[c, peer],
            send_sem=send2.at[c, peer], recv_sem=recv2.at[c, peer],
            device_id=(peer, lane), device_id_type=MESH,
        )

    for i, k in enumerate(order):
        if i:
            mix(i)
        out_copy(0, k).start()
    for c in range(1, chunks):
        for k in order:
            out_copy(c, k).start()
    for load in loads:
        load.start()
    mix(n - 1)
    for c in range(chunks):
        data[c, me] = mixed[c, me]

    loads[0].wait()
    loads[1].wait()
    hidden = jnp.tanh(jnp.dot(feats_ref[...], pos_ref[...], precision=HIGHEST, preferred_element_type=jnp.float32))
    loads[2].wait()
    loads[3].wait()
    rates = rates_ref[...]
    gain = jnp.sqrt(2.0 * rates)
    for i in range(n):
        part = hidden[i * rows:(i + 1) * rows]
        profile = jnp.dot(part, weight_buf[...], precision=HIGHEST, preferred_element_type=jnp.float32)
        time = (lax.broadcasted_iota(jnp.int32, (rows, width), 0) + i * rows).astype(jnp.float32)
        taps[pl.ds(i * rows, rows), :] = (jnp.exp(-rates * time) * gain * profile).astype(jnp.bfloat16)
    loads[4].wait()

    @pl.loop(0, length // block)
    def _(b):
        at = pl.ds(pl.multiple_of(b * 2 * block, 2 * block), 2 * block)
        filt_spec[at, :] = jnp.dot(fwd_buf[at, :], taps[...], preferred_element_type=jnp.float32)

    loads[5].wait()
    for c in range(chunks):
        for k in order:
            in_copy(c, k).wait_recv()
        held = data.at[c]

        @pl.loop(0, length // block)
        def _(b):
            at = pl.ds(pl.multiple_of(b * 2 * block, 2 * block), 2 * block)
            x = jnp.dot(fwd_buf[at, :], held[...].reshape(length, LANES), preferred_element_type=jnp.float32)
            h = filt_spec[at, pl.ds(c * LANES, LANES)]
            xc, xs, hc, hs = x[:block], x[block:], h[:block], h[block:]
            both = jnp.concatenate([xc * hc - xs * hs, xc * hs + xs * hc], axis=0)
            spec[at, :] = both.astype(jnp.bfloat16)

        pairs = n // 2
        for step in [(pairs // 2 + i) % pairs for i in range(pairs)]:
            pair = lax.rem(me // 2 + step, pairs)
            at = pl.ds(pl.multiple_of(pair * 2 * rows, 2 * rows), 2 * rows)
            part = jnp.dot(bwd_buf[at, :], spec[...], preferred_element_type=jnp.float32)
            conv[c, pl.ds(pair * 2, 2)] = part.astype(jnp.bfloat16).reshape(2, rows, LANES)
            if step:
                for half in range(2):
                    out_back(c, pair * 2 + half).start()
            else:
                out_back(c, pair * 2 + 1 - lax.rem(me, 2)).start()
        back[c, me] = conv[c, me]

    loads[6].wait()
    loads[7].wait()
    squares = jnp.zeros((rows, LANES), jnp.float32)
    for c in range(chunks):
        for k in [0] + order[::-1]:
            peer = seq_peer(k)
            if k:
                in_back(c, peer).wait_recv()
            at = pl.ds(pl.multiple_of(peer * width + c * LANES, LANES), LANES)
            total = back[c, peer].astype(jnp.float32) + skip_ref[:, at] * mixed[c, peer].astype(jnp.float32)
            gated = q_buf[:, at].astype(jnp.float32) * total
            gated_ref[:, at] = gated
            squares = squares + gated * gated
    eye = lax.broadcasted_iota(jnp.int32, (rows, LANES), 0) == lax.broadcasted_iota(jnp.int32, (rows, LANES), 1)
    column = jnp.sum(squares, axis=1, keepdims=True)
    line = jnp.sum(jnp.where(eye, column, 0.0), axis=0, keepdims=True)
    sums_out[...] = jnp.broadcast_to(line, sums_out.shape)

    def sums_copy(k, mine):
        peer = lax.rem(lane + k, m)
        slot = lane if mine else peer
        return pltpu.make_async_remote_copy(
            src_ref=sums_out, dst_ref=sums_in.at[slot],
            send_sem=send3.at[peer], recv_sem=recv3.at[slot],
            device_id=(me, peer), device_id_type=MESH,
        )

    for k in range(1, m):
        sums_copy(k, True).start()
    total = sums_out[...]
    for k in range(1, m):
        sums_copy(k, False).wait_recv()
        total = total + sums_in[lax.rem(lane + k, m)]
    inv = lax.rsqrt(total[:1] / (cols * m) + 1e-06)
    inv = jnp.sum(jnp.where(eye, inv, 0.0), axis=1, keepdims=True)
    loads[8].wait()
    stores = []
    for d in range(n):
        at = pl.ds(d * width, width)
        gated_ref[:, at] = gated_ref[:, at] * inv * gain_ref[:, at]
        stores.append(pltpu.make_async_copy(gated_ref.at[:, at], out_hbm.at[:, at], out_sem.at[d]))
        stores[-1].start()

    for c in range(chunks):
        for k in order:
            out_copy(c, k).wait_send()
            out_back(c, seq_peer(k)).wait_send()
    for k in range(1, m):
        sums_copy(k, True).wait_send()
    for store in stores:
        store.wait()


def fused(queries, key_in, values, decay_rates, skip_gain, out_gain, pos_weight, filt_weight):
    rows, cols = queries.shape
    n, m = lax.axis_size("seq"), lax.axis_size("chan")
    length, width = rows * n, cols // n
    chunks = width // LANES
    block = min(2 * LANES, length)
    forward, backward = (jnp.asarray(t) for t in spectral_tables(length, block))
    hbm = pl.BlockSpec(memory_space=pltpu.HBM)
    bf16, f32 = jnp.bfloat16, jnp.float32
    dma = pltpu.SemaphoreType.DMA
    return pl.pallas_call(
        functools.partial(kernel, n, m, block),
        out_shape=jax.ShapeDtypeStruct((rows, cols), f32),
        in_specs=[hbm] * 11,
        out_specs=hbm,
        scratch_shapes=[
            pltpu.VMEM((rows, cols), bf16),
            pltpu.VMEM((rows, cols), bf16),
            pltpu.VMEM((rows, cols), bf16),
            pltpu.VMEM((1, width), f32),
            pltpu.VMEM((1, cols), f32),
            pltpu.VMEM((1, cols), f32),
            pltpu.VMEM((length, 2 * FREQS), f32),
            pltpu.VMEM(pos_weight.shape, f32),
            pltpu.VMEM((filt_weight.shape[0], width), f32),
            pltpu.VMEM((2 * length, length), bf16),
            pltpu.VMEM((length, 2 * length), bf16),
            pltpu.VMEM((chunks, n, rows, LANES), bf16),
            pltpu.VMEM((chunks, n, rows, LANES), bf16),
            pltpu.VMEM((length, width), bf16),
            pltpu.VMEM((2 * length, width), f32),
            pltpu.VMEM((2 * length, LANES), bf16),
            pltpu.VMEM((chunks, n, rows, LANES), bf16),
            pltpu.VMEM((chunks, n, rows, LANES), bf16),
            pltpu.VMEM((8, LANES), f32),
            pltpu.VMEM((m, 8, LANES), f32),
            pltpu.VMEM((rows, cols), f32),
            dma((9,)),
            dma((n,)),
            dma((n,)),
            dma((n,)),
            dma((chunks, n)),
            dma((chunks, n)),
            dma((chunks, n)),
            dma((chunks, n)),
            dma((m,)),
            dma((m,)),
        ],
        compiler_params=pltpu.CompilerParams(
            collective_id=0, has_side_effects=True, vmem_limit_bytes=63 * 1024 * 1024
        ),
    )(
        queries, key_in, values, decay_rates[None, :], skip_gain[None, :], out_gain[None, :],
        jnp.asarray(feature_table(length)), pos_weight, filt_weight, forward, backward,
    )


def local(queries, *others):
    rows, cols = queries.shape
    n = lax.axis_size("seq")
    if rows == LANES and n % 4 == 0 and cols % (LANES * n) == 0:
        return fused(queries, *others)
    return plain(queries, *others)


def solution(mesh):
    in_specs = (
        P("seq", "chan"),
        P("seq", "chan"),
        P("seq", "chan"),
        P("chan"),
        P("chan"),
        P("chan"),
        P(),
        P(None, "chan"),
    )
    return jax.shard_map(
        local, mesh=mesh, in_specs=in_specs, out_specs=P("seq", "chan"), check_vma=False
    )
```
